128 devices in a mesh: section: 2 (over core), dp: 8 (over y_lo, z), tensor: 8 (over x, y_hi).
Axes of the slice: x: 4, y: 4 (y_hi: 2, y_lo: 2; y = y_hi * 2 + y_lo), z: 4, core: 2. Of those that a mesh axis runs over, the one named last changes fastest.
Arguments:
- context: bfloat16 [2, 2048, 6144], P(None, 'dp', ('section', 'tensor')), may hold values from -6 to 6
- residual: bfloat16 [2, 2048, 9216], P(None, 'dp', ('section', 'tensor')), may hold values from -6 to 6
- out_weight: bfloat16 [6144, 9216], P(('section', 'tensor')), may hold values from -0.109375 to 0.109375
- out_bias: float32 [9216], P(('section', 'tensor')), may hold values from -3 to 3
- norm_gain: float32 [9216], replicated, may hold values from 0.1 to 1.9
- norm_bias: float32 [9216], replicated, may hold values from -3 to 3
- query_weight: bfloat16 [9216, 6144], P(None, 'tensor'), may hold values from -0.0625 to 0.0625
- query_bias: float32 [6144], P('tensor'), may hold values from -3 to 3
- grad_handoff: bfloat16 [2, 2048, 9216], P('section', ('dp', 'tensor')), may hold values from -16 to 16
Outputs:
- query: bfloat16 [2, 2048, 6144], P('section', 'dp', 'tensor')
- grad_context: bfloat16 [2, 2048, 6144], P(None, 'dp', ('section', 'tensor'))
- grad_out_weight: bfloat16 [6144, 9216], P(('section', 'tensor'), 'dp')
The draws below stay inside these ranges and needn't reach their ends.
All inputs are finite; a program needn't handle non-finite values.
Results may differ from the reference program's by a relative error of at most 0.017.
Values may be sent and summed in bfloat16 or wider, within the bound.
A program may use at most 128 MiB of HBM per device.

```python
import jax
import jax.numpy as jnp
from jax import lax

D = 9216
SEQS = 2
LEN = 2048
HD = 6144
N_SECTION = 2
N_DP = 8
N_TENSOR = 8


def with_spikes(values, rng, source, target, shards_of, factor):
    def block_of(dim):
        return (jnp.arange(values.shape[dim]) // (values.shape[dim] // shards_of)).reshape((-1,) + (1,) * (values.ndim - 1 - dim))

    one_side = jax.random.permutation(rng, shards_of)[block_of(target)]
    other_side = (block_of(target) + shards_of // 2) % shards_of
    return jnp.where((block_of(source) == one_side) | (block_of(source) == other_side), factor * values, values)


def levels(stream_key, extent, cuts, least, high):
    factor_of, own = 1.0, jax.random.fold_in(stream_key, 6)
    for axis_at, parts in cuts:
        steps = jnp.exp(jax.random.uniform(jax.random.fold_in(own, axis_at), (parts,), jnp.float32, least / len(cuts), high / len(cuts)))
        factor_of = factor_of * jnp.repeat(steps, extent[axis_at] // parts).reshape([-1 if axis == axis_at else 1 for axis in range(len(extent))])
    return factor_of


def scatter_about(rng, extent, spread, limit, shards=(), held_as=jnp.bfloat16):
    gain = levels(rng, extent, shards, -0.22, 0.18) if shards else 1.0
    entries = jax.random.normal(rng, extent, jnp.float32) * spread * gain
    return jnp.minimum(jnp.maximum(entries, -limit), limit).astype(held_as)


def gaussian_with(key, dims, scale, limit, cuts, heavy, kind=jnp.bfloat16):
    result = scale * jax.random.normal(key, dims, jnp.float32)
    if cuts:
        result = result * levels(key, dims, cuts, -0.22, 0.18)
    return jnp.clip(with_spikes(result, jax.random.fold_in(key, 3), *heavy), -limit, limit).astype(kind)


def setup_inputs(seed: int = 0) -> dict:
    streams_of = jax.random.split(jax.random.key(seed), 10)
    context = scatter_about(streams_of[0], (SEQS, LEN, HD), 1.0, 6.0, ((1, 8), (2, 16)))
    residual = scatter_about(streams_of[1], (SEQS, LEN, D), 1.0, 6.0, ((1, 8), (2, 16)))
    out_weight = gaussian_with(streams_of[2], (HD, D), HD ** -0.5, 0.109375, ((0, 16),), (0, 1, 16, 2.0))
    out_bias = scatter_about(streams_of[3], (D,), 0.5, 3.0, ((0, 16),), jnp.float32)
    norm_gain = jnp.clip(1.0 + 0.18 * jax.random.normal(streams_of[4], (D,), jnp.float32), 0.1, 1.9)
    norm_bias = scatter_about(streams_of[5], (D,), 0.5, 3.0, (), jnp.float32)
    query_weight = scatter_about(streams_of[6], (D, HD), D ** -0.5, 0.0625, ((1, 8),))
    query_bias = scatter_about(streams_of[7], (HD,), 0.5, 3.0, ((0, 8),), jnp.float32)
    grad_handoff = gaussian_with(streams_of[8], (SEQS, LEN, D), 1.0, 16.0, ((0, 2), (1, 64)), (1, 2, 64, 4.0))
    return {"context": context, "residual": residual, "out_weight": out_weight, "out_bias": out_bias, "norm_gain": norm_gain, "norm_bias": norm_bias, "query_weight": query_weight, "query_bias": query_bias, "grad_handoff": grad_handoff}


epsilon = 1e-05

def reference(context, residual, out_weight, out_bias, norm_gain, norm_bias, query_weight, query_bias, grad_handoff):
    blocks = N_SECTION * N_TENSOR
    head_cols = HD // blocks
    row_count = SEQS * LEN
    context_blocks = context.reshape(row_count, blocks, head_cols)

    def add_block(running, block_index):
        ctx_block = lax.dynamic_slice_in_dim(context_blocks, block_index, 1, 1).reshape(row_count, head_cols)
        weight_block = lax.dynamic_slice_in_dim(out_weight, block_index * head_cols, head_cols, 0)
        partial_value = jnp.dot(ctx_block, weight_block, preferred_element_type=jnp.float32).astype(jnp.bfloat16)
        partial_value = lax.optimization_barrier(partial_value)
        return (running + partial_value.astype(jnp.float32), None)
    proj, _ = lax.scan(add_block, jnp.zeros((row_count, D), jnp.float32), jnp.arange(blocks, dtype=jnp.int32))
    handoff = (residual.reshape(row_count, D).astype(jnp.float32) + proj + out_bias).astype(jnp.bfloat16)
    wide = handoff.astype(jnp.float32)
    mean_value = lax.optimization_barrier(jnp.mean(wide, axis=-1, keepdims=True))
    centred = wide - mean_value
    variance = lax.optimization_barrier(jnp.mean(centred * centred, axis=-1, keepdims=True))
    normed = (centred * lax.rsqrt(variance + epsilon) * norm_gain + norm_bias).astype(jnp.bfloat16)
    query = (jnp.dot(normed, query_weight, preferred_element_type=jnp.float32) + query_bias).astype(jnp.bfloat16)
    query = query.reshape(SEQS, LEN, HD)
    grad_rows = grad_handoff.reshape(row_count, D)
    grad_context = jnp.dot(grad_rows, out_weight.T, preferred_element_type=jnp.float32).astype(jnp.bfloat16)
    grad_context = grad_context.reshape(SEQS, LEN, HD)
    block_len = LEN // N_DP

    def add_rows(running, block_index):
        ctx_block = lax.dynamic_slice_in_dim(context, block_index * block_len, block_len, 1).reshape(SEQS * block_len, HD)
        grad_block = lax.dynamic_slice_in_dim(grad_handoff, block_index * block_len, block_len, 1).reshape(SEQS * block_len, D)
        partial_value = jnp.dot(ctx_block.T, grad_block, preferred_element_type=jnp.float32).astype(jnp.bfloat16)
        partial_value = lax.optimization_barrier(partial_value)
        return (running + partial_value.astype(jnp.float32), None)
    weight_total, _ = lax.scan(add_rows, jnp.zeros((HD, D), jnp.float32), jnp.arange(N_DP, dtype=jnp.int32))
    return (query, grad_context, weight_total.astype(jnp.bfloat16))
```

```python
import jax
import jax.numpy as jnp
from jax import lax
from jax.experimental import pallas as pl
from jax.experimental.pallas import tpu as pltpu
from jax.sharding import PartitionSpec as P

EPSILON = 1e-05
MESH = pl.DeviceIdType.MESH
BF16 = jnp.bfloat16
F32 = jnp.float32

CHUNKS = 8
CW = 1152
WIDTH = CHUNKS * CW
SEQ_ROWS = 256
PIECE = 32
HEADS = 384
HALF = HEADS // 2
QCOLS = 768
WQ_SLOTS = 3

STAGES = {
    "g1": (0, 2),
    "p1": (0, 1),
    "p2": (1, 1),
    "p3": (3, 1),
    "p4": (5, 1),
    "p5": (7, 1),
    "g2": (2, 2),
    "g3": (3, 2),
    "g4": (5, 2),
    "c": (6, 2),
    "w2": (8, 2),
    "n2": (15, 1),
    "n3": (16, 1),
    "q": (18, 1),
}
LN_TICK = 14
TICKS = 26


def wait_for(ref, sem):
    pltpu.make_async_copy(ref, ref, sem).wait()


def kernel(
    ctx_hbm, res_hbm, ow_hbm, bias_ref, gain_ref, nbias_ref, qw_hbm, qbias_ref, grad_hbm,
    query_ref, gctx_ref, gow_ref,
    ctx, ctxt, res, wv, xsend, xbuf, pbuf, s1r, s1l, finl, finr, ybuf, hbuf,
    wq, gbuf, wbuf, ws1r, ws1l, wfinl, wfinr, wy, gacc, qacc, rowsum,
    in_sem, wv_sem, wq_sem, gin_sem,
    xsend_sem, xrecv_sem, p_send, s1r_sem, s1l_sem, finl_sem, finr_sem, y_sem,
    g_send, gc_send, g_sem, gc_sem, n_send, n_sem,
    w_send, ws1_send, ws1r_sem, ws1l_sem, wfinl_sem, wfinr_sem, wy_send, wy_sem,
):
    s = lax.axis_index("section")
    d = lax.axis_index("dp")
    t = lax.axis_index("tensor")
    x, yh = t // 2, t % 2
    yl, z = d // 4, d % 4
    other_core = (1 - s, d, t)
    xr = (s, d, ((x + 1) % 4) * 2 + yh)
    xl = (s, d, ((x + 3) % 4) * 2 + yh)
    ypart = (s, d, x * 2 + (1 - yh))
    zr = (s, yl * 4 + (z + 1) % 4, t)
    zl = (s, yl * 4 + (z + 3) % 4, t)
    pair = (s, (1 - yl) * 4 + z, t)

    def send(src, dst, ssem, rsem, to):
        pltpu.make_async_remote_copy(
            src_ref=src, dst_ref=dst, send_sem=ssem, recv_sem=rsem, device_id=to, device_id_type=MESH
        ).start()

    def own_rows(offset):
        return pl.ds(((x + offset) % 4) * 64 + yh * PIECE, PIECE)

    def far_rows(offset):
        return pl.ds(((x + offset) % 4) * 64 + (1 - yh) * PIECE, PIECE)

    ctx_load = pltpu.make_async_copy(ctx_hbm, ctx, in_sem.at[0])
    ctx_load.start()

    def wv_load(c):
        return pltpu.make_async_copy(
            ow_hbm.at[:, pl.ds(pl.multiple_of(c * CW, 128), CW)], wv.at[c], wv_sem.at[c]
        )

    def gin_load(c):
        return pltpu.make_async_copy(
            grad_hbm.at[:, pl.ds(pl.multiple_of(c * CW, 128), CW)],
            gbuf.at[c, pl.ds(s * SEQ_ROWS + t * PIECE, PIECE)],
            gin_sem.at[c],
        )

    def wq_load(c):
        return pltpu.make_async_copy(
            qw_hbm.at[pl.ds(c * CW, CW)], wq.at[c % WQ_SLOTS], wq_sem.at[c % WQ_SLOTS]
        )

    wv_load(0).start()

    @pl.loop(0, CHUNKS)
    def _(c):
        gin_load(c).start()

    res_load = pltpu.make_async_copy(res_hbm, res, in_sem.at[1])
    res_load.start()

    @pl.loop(1, CHUNKS)
    def _(c):
        wv_load(c).start()

    @pl.loop(0, WQ_SLOTS)
    def _(c):
        wq_load(c).start()

    barrier = pltpu.get_barrier_semaphore()
    neighbours = (other_core, xr, xl, ypart, zr, zl, pair)
    for to in neighbours:
        pl.semaphore_signal(barrier, inc=1, device_id=to, device_id_type=MESH)

    ctx_load.wait()
    ctxt[...] = ctx[...].T
    gacc[...] = jnp.zeros_like(gacc)
    qacc[...] = jnp.zeros_like(qacc)
    rowsum[...] = jnp.zeros_like(rowsum)
    res_load.wait()

    @pl.loop(0, CHUNKS)
    def _(c):
        gin_load(c).wait()

    pl.semaphore_wait(barrier, len(neighbours))

    res_chunk = 4 * s + x

    def p1(c):
        slot = c % 2

        @pl.when(c < 4)
        def _():
            wv_load(c).wait()

        @pl.when(c == 4)
        def _():
            for later in range(4, CHUNKS):
                wv_load(later).wait()

        @pl.when(c >= 2)
        def _():
            wait_for(xsend.at[slot], xsend_sem.at[slot])

        rows = pl.ds((1 - s) * SEQ_ROWS, SEQ_ROWS)
        part = jnp.dot(ctx[rows], wv[c], preferred_element_type=F32)

        @pl.when(c == res_chunk)
        def _():
            xsend[slot] = (part + res[rows].astype(F32) + bias_ref[...]).astype(BF16)

        @pl.when(c != res_chunk)
        def _():
            xsend[slot] = part.astype(BF16)

        send(xsend.at[slot], xbuf.at[c], xsend_sem.at[slot], xrecv_sem.at[c], other_core)

    def p2(c):
        rows = pl.ds(s * SEQ_ROWS, SEQ_ROWS)
        part = jnp.dot(ctx[rows], wv[c], preferred_element_type=F32)
        wait_for(xbuf.at[c], xrecv_sem.at[c])

        @pl.when(c == res_chunk)
        def _():
            pbuf[c] = (part + xbuf[c].astype(F32) + res[rows].astype(F32) + bias_ref[...]).astype(BF16)

        @pl.when(c != res_chunk)
        def _():
            pbuf[c] = (part + xbuf[c].astype(F32)).astype(BF16)

        send(pbuf.at[c, far_rows(2)], s1r.at[c], p_send, s1r_sem.at[c], xr)
        send(pbuf.at[c, own_rows(2)], s1l.at[c], p_send, s1l_sem.at[c], xl)
        send(pbuf.at[c, own_rows(1)], finl.at[c, 0], p_send, finl_sem.at[c, 0], xr)
        send(pbuf.at[c, far_rows(3)], finr.at[c, 1], p_send, finr_sem.at[c, 1], xl)

    def p3(c):
        wait_for(s1r.at[c], s1r_sem.at[c])
        rows = far_rows(1)
        pbuf[c, rows] = (pbuf[c, rows].astype(F32) + s1r[c].astype(F32)).astype(BF16)
        send(pbuf.at[c, rows], finl.at[c, 1], p_send, finl_sem.at[c, 1], xr)
        wait_for(s1l.at[c], s1l_sem.at[c])
        rows = own_rows(3)
        pbuf[c, rows] = (pbuf[c, rows].astype(F32) + s1l[c].astype(F32)).astype(BF16)
        send(pbuf.at[c, rows], finr.at[c, 0], p_send, finr_sem.at[c, 0], xl)

    def p4(c):
        wait_for(finl.at[c, 1], finl_sem.at[c, 1])
        wait_for(finr.at[c, 1], finr_sem.at[c, 1])
        rows = far_rows(0)
        pbuf[c, rows] = (
            pbuf[c, rows].astype(F32) + finl[c, 1].astype(F32) + finr[c, 1].astype(F32)
        ).astype(BF16)
        send(pbuf.at[c, rows], ybuf.at[c], p_send, y_sem.at[c], ypart)

    def p5(c):
        wait_for(finl.at[c, 0], finl_sem.at[c, 0])
        wait_for(finr.at[c, 0], finr_sem.at[c, 0])
        wait_for(ybuf.at[c], y_sem.at[c])
        total = (
            pbuf[c, own_rows(0)].astype(F32)
            + finl[c, 0].astype(F32)
            + finr[c, 0].astype(F32)
            + ybuf[c].astype(F32)
        )
        handoff = total.astype(BF16)
        hbuf[c] = handoff
        rowsum[...] += jnp.sum(handoff.astype(F32), axis=-1, keepdims=True)

    def gather1(buf, c, base, sems, ssem):
        rows = own_rows(0)
        rows = pl.ds(base + rows.start, PIECE)
        send(buf.at[c, rows], buf.at[c, rows], ssem, sems.at[c, 0], ypart)
        send(buf.at[c, rows], buf.at[c, rows], ssem, sems.at[c, 1], xr)
        send(buf.at[c, rows], buf.at[c, rows], ssem, sems.at[c, 2], xl)

    def shifted(rows, base):
        return pl.ds(base + rows.start, PIECE)

    def gather2(buf, c, base, sems, ssem):
        rows = shifted(own_rows(3), base)
        wait_for(buf.at[c, rows], sems.at[c, 1])
        send(buf.at[c, rows], buf.at[c, rows], ssem, sems.at[c, 5], xr)
        rows = shifted(far_rows(0), base)
        wait_for(buf.at[c, rows], sems.at[c, 0])
        send(buf.at[c, rows], buf.at[c, rows], ssem, sems.at[c, 4], xl)
        send(buf.at[c, rows], buf.at[c, rows], ssem, sems.at[c, 3], xr)

    def gather3(buf, c, base, sems, ssem):
        rows = shifted(far_rows(1), base)
        wait_for(buf.at[c, rows], sems.at[c, 4])
        send(buf.at[c, rows], buf.at[c, rows], ssem, sems.at[c, 6], xl)

    def gather4(buf, c, base, sems):
        wait_for(buf.at[c, shifted(own_rows(1), base)], sems.at[c, 2])
        wait_for(buf.at[c, shifted(far_rows(3), base)], sems.at[c, 3])
        wait_for(buf.at[c, shifted(own_rows(2), base)], sems.at[c, 5])
        wait_for(buf.at[c, shifted(far_rows(2), base)], sems.at[c, 6])

    def order(j):
        near = j % 2
        ring = (j + 2) // 4
        mid = ring % 2
        step = (2 + ring * (3 + 2 * near)) % 4
        own = near + mid * ((j + 2) // 2 - 2 - near)
        half = (yl + 1 + own) % 2
        return half * 4 + (z + step) % 4, own

    g_base = s * SEQ_ROWS

    def g1(j):
        gather1(gbuf, order(j)[0], g_base, g_sem, g_send)

    def g2(j):
        gather2(gbuf, order(j)[0], g_base, g_sem, g_send)

    def g3(j):
        gather3(gbuf, order(j)[0], g_base, g_sem, g_send)

    def g4(j):
        c = order(j)[0]
        gather4(gbuf, c, g_base, g_sem)
        rows = pl.ds(g_base, SEQ_ROWS)
        send(gbuf.at[c, rows], gbuf.at[c, rows], gc_send, gc_sem.at[c], other_core)

    def compute(j):
        c, own = order(j)
        rows = pl.ds((1 - s) * SEQ_ROWS, SEQ_ROWS)
        wait_for(gbuf.at[c, rows], gc_sem.at[c])
        slot = j % 6

        @pl.when(j >= 6)
        def _():
            wait_for(wbuf.at[slot], ws1_send.at[slot])

        term = jnp.dot(ctxt[...], gbuf[c], preferred_element_type=F32).astype(BF16)
        wbuf[slot, 0] = term[:HALF]
        wbuf[slot, 1] = term[HALF:]

        @pl.when(j < 2)
        def _():
            send(wbuf.at[slot, 0], ws1r.at[own], ws1_send.at[slot], ws1r_sem.at[own], zr)
            send(wbuf.at[slot, 1], ws1l.at[own], ws1_send.at[slot], ws1l_sem.at[own], zl)

        @pl.when((j >= 2) & (j < 6) & (j % 2 == 0))
        def _():
            send(wbuf.at[slot, 1], wfinl.at[own, 1], w_send, wfinl_sem.at[own, 1], zr)

        @pl.when((j >= 2) & (j < 6) & (j % 2 == 1))
        def _():
            send(wbuf.at[slot, 0], wfinr.at[own, 0], w_send, wfinr_sem.at[own, 0], zl)

        gacc[...] += lax.dot_general(
            gbuf[c], wv[c], (((1,), (1,)), ((), ())), preferred_element_type=F32
        )

    def w2(j):
        own = order(j)[1]

        @pl.when((j >= 2) & (j < 6) & (j % 2 == 0))
        def _():
            wait_for(ws1r.at[own], ws1r_sem.at[own])
            wbuf[j, 0] = (wbuf[j, 0].astype(F32) + ws1r[own].astype(F32)).astype(BF16)
            send(wbuf.at[j, 0], wfinl.at[own, 0], w_send, wfinl_sem.at[own, 0], zr)

        @pl.when((j >= 2) & (j < 6) & (j % 2 == 1))
        def _():
            wait_for(ws1l.at[own], ws1l_sem.at[own])
            wbuf[j, 1] = (wbuf[j, 1].astype(F32) + ws1l[own].astype(F32)).astype(BF16)
            send(wbuf.at[j, 1], wfinr.at[own, 1], w_send, wfinr_sem.at[own, 1], zl)

    def norm():
        mean = rowsum[...] * (1.0 / WIDTH)

        def square(c, total):
            centred = hbuf[c].astype(F32) - mean
            return total + jnp.sum(centred * centred, axis=-1, keepdims=True)

        total = lax.fori_loop(0, CHUNKS, square, jnp.zeros((PIECE, 1), F32))
        scale = lax.rsqrt(total * (1.0 / WIDTH) + EPSILON)

        @pl.loop(0, CHUNKS)
        def _(c):
            centred = hbuf[c].astype(F32) - mean
            gain = gain_ref[pl.ds(c, 1), :]
            shift = nbias_ref[pl.ds(c, 1), :]
            xbuf[c, own_rows(0)] = (centred * scale * gain + shift).astype(BF16)
            gather1(xbuf, c, 0, n_sem, n_send)

    def n2(c):
        gather2(xbuf, c, 0, n_sem, n_send)

    def n3(c):
        gather3(xbuf, c, 0, n_sem, n_send)

    def q(c):
        gather4(xbuf, c, 0, n_sem)
        wq_load(c).wait()
        qacc[...] += jnp.dot(xbuf[c], wq[c % WQ_SLOTS], preferred_element_type=F32)

        @pl.when(c + WQ_SLOTS < CHUNKS)
        def _():
            wq_load(c + WQ_SLOTS).start()

    bodies = {
        "g1": g1, "p1": p1, "p2": p2, "p3": p3, "p4": p4, "p5": p5, "g2": g2, "g3": g3, "g4": g4,
        "c": compute, "w2": w2, "n2": n2, "n3": n3, "q": q,
    }

    @pl.loop(0, TICKS)
    def _(k):
        for name, (first, stride) in STAGES.items():
            if name == "n2":

                @pl.when(k == LN_TICK)
                def _():
                    norm()

            index = (k - first) // stride

            @pl.when((k >= first) & (k < first + CHUNKS * stride) & ((k - first) % stride == 0))
            def _():
                bodies[name](index)

    gctx_ref[...] = gacc[...].astype(BF16)
    query_ref[...] = (qacc[...] + qbias_ref[...]).astype(BF16)

    for half in range(2):
        wait_for(wfinl.at[0, half], wfinl_sem.at[0, half])
        wait_for(wfinr.at[0, half], wfinr_sem.at[0, half])
        wbuf[0, half] = (
            wbuf[0, half].astype(F32) + wfinl[0, half].astype(F32) + wfinr[0, half].astype(F32)
        ).astype(BF16)
        send(wbuf.at[0, half], wy.at[half], wy_send.at[half], wy_sem.at[half], pair)
    for half in range(2):
        wait_for(wfinl.at[1, half], wfinl_sem.at[1, half])
        wait_for(wfinr.at[1, half], wfinr_sem.at[1, half])
        wait_for(wy.at[half], wy_sem.at[half])
        gow_ref[half] = (
            wbuf[1, half].astype(F32)
            + wfinl[1, half].astype(F32)
            + wfinr[1, half].astype(F32)
            + wy[half].astype(F32)
        ).astype(BF16)

    for slot in range(2):
        wait_for(xsend.at[slot], xsend_sem.at[slot])
        wait_for(wy.at[slot], wy_send.at[slot])
    wait_for(pbuf.at[:, pl.ds(0, 224)], p_send)
    wait_for(gbuf.at[:, pl.ds(0, 224)], g_send)
    wait_for(gbuf.at[:, pl.ds(0, 256)], gc_send)
    wait_for(xbuf.at[:, pl.ds(0, 224)], n_send)
    wait_for(wbuf.at[pl.ds(2, 4)], w_send)


def local(
    context, residual, out_weight, out_bias, norm_gain, norm_bias, query_weight, query_bias, grad_handoff
):
    t = lax.axis_index("tensor")
    rows = 2 * SEQ_ROWS
    feats = WIDTH // 16
    ctx = context.reshape(rows, HEADS)
    res = residual.reshape(rows, feats)
    even = t % 2 == 0

    def place(a):
        zero = jnp.zeros_like(a)
        return jnp.where(
            even, jnp.concatenate([a, zero], axis=1), jnp.concatenate([zero, a], axis=1)
        )

    dma = pltpu.SemaphoreType.DMA
    any_spec = pl.BlockSpec(memory_space=pl.ANY)
    vmem_spec = pl.BlockSpec(memory_space=pltpu.VMEM)
    query, gctx, gow = pl.pallas_call(
        kernel,
        out_shape=(
            jax.ShapeDtypeStruct((SEQ_ROWS, QCOLS), BF16),
            jax.ShapeDtypeStruct((rows, HEADS), BF16),
            jax.ShapeDtypeStruct((2, HALF, CW), BF16),
        ),
        in_specs=[any_spec, any_spec, any_spec, vmem_spec, vmem_spec, vmem_spec, any_spec, vmem_spec, any_spec],
        out_specs=(vmem_spec, vmem_spec, vmem_spec),
        scratch_shapes=[
            pltpu.VMEM((rows, HEADS), BF16),
            pltpu.VMEM((HEADS, rows), BF16),
            pltpu.VMEM((rows, CW), BF16),
            pltpu.VMEM((CHUNKS, HEADS, CW), BF16),
            pltpu.VMEM((2, SEQ_ROWS, CW), BF16),
            pltpu.VMEM((CHUNKS, SEQ_ROWS, CW), BF16),
            pltpu.VMEM((CHUNKS, SEQ_ROWS, CW), BF16),
            pltpu.VMEM((CHUNKS, PIECE, CW), BF16),
            pltpu.VMEM((CHUNKS, PIECE, CW), BF16),
            pltpu.VMEM((CHUNKS, 2, PIECE, CW), BF16),
            pltpu.VMEM((CHUNKS, 2, PIECE, CW), BF16),
            pltpu.VMEM((CHUNKS, PIECE, CW), BF16),
            pltpu.VMEM((CHUNKS, PIECE, CW), BF16),
            pltpu.VMEM((WQ_SLOTS, CW, QCOLS), BF16),
            pltpu.VMEM((CHUNKS, rows, CW), BF16),
            pltpu.VMEM((6, 2, HALF, CW), BF16),
            pltpu.VMEM((2, HALF, CW), BF16),
            pltpu.VMEM((2, HALF, CW), BF16),
            pltpu.VMEM((2, 2, HALF, CW), BF16),
            pltpu.VMEM((2, 2, HALF, CW), BF16),
            pltpu.VMEM((2, HALF, CW), BF16),
            pltpu.VMEM((rows, HEADS), F32),
            pltpu.VMEM((SEQ_ROWS, QCOLS), F32),
            pltpu.VMEM((PIECE, 1), F32),
            dma((2,)),
            dma((CHUNKS,)),
            dma((WQ_SLOTS,)),
            dma((CHUNKS,)),
            dma((2,)),
            dma((CHUNKS,)),
            dma,
            dma((CHUNKS,)),
            dma((CHUNKS,)),
            dma((CHUNKS, 2)),
            dma((CHUNKS, 2)),
            dma((CHUNKS,)),
            dma,
            dma,
            dma((CHUNKS, 7)),
            dma((CHUNKS,)),
            dma,
            dma((CHUNKS, 7)),
            dma,
            dma((2,)),
            dma((2,)),
            dma((2,)),
            dma((2, 2)),
            dma((2, 2)),
            dma((2,)),
            dma((2,)),
        ],
        compiler_params=pltpu.CompilerParams(
            collective_id=0, has_side_effects=True, vmem_limit_bytes=62 * 2**20
        ),
    )(
        ctx,
        place(res),
        out_weight,
        place(out_bias.reshape(1, feats)),
        norm_gain.reshape(CHUNKS, CW),
        norm_bias.reshape(CHUNKS, CW),
        query_weight,
        query_bias.reshape(1, QCOLS),
        grad_handoff.reshape(PIECE, WIDTH),
    )
    return (
        query.reshape(1, SEQ_ROWS, QCOLS),
        gctx.reshape(2, SEQ_ROWS, HEADS),
        gow.reshape(HEADS, CW),
    )


def solution(mesh):
    in_specs = (
        P(None, "dp", ("section", "tensor")),
        P(None, "dp", ("section", "tensor")),
        P(("section", "tensor"), None),
        P(("section", "tensor")),
        P(),
        P(),
        P(None, "tensor"),
        P("tensor"),
        P("section", ("dp", "tensor"), None),
    )
    out_specs = (
        P("section", "dp", "tensor"),
        P(None, "dp", ("section", "tensor")),
        P(("section", "tensor"), "dp"),
    )
    return jax.shard_map(local, mesh=mesh, in_specs=in_specs, out_specs=out_specs, check_vma=False)
```

```python
import jax
import jax.numpy as jnp
from jax import lax
from jax.experimental import pallas as pl
from jax.experimental.pallas import tpu as pltpu
from jax.sharding import PartitionSpec as P

EPSILON = 1e-05
MESH = pl.DeviceIdType.MESH
BF16 = jnp.bfloat16
F32 = jnp.float32

CHUNKS = 8
CW = 1152
WIDTH = CHUNKS * CW
FEATS = WIDTH // 16
SEQ_ROWS = 256
PIECE = 32
SUB = 16
UNITS = 8
HEADS = 384
HALF = HEADS // 2
QCOLS = 768
WQ_SLOTS = 2

SCHEDULE = {
    "g1": (0, 1, 2, 3, 4, 5, 6, 7),
    "c": (20, 21, 27, 29, 31, 37, 38, 44),
    "n2": (38, 39, 40, 41, 45, 46, 47, 49),
    "p3": (11, 13, 15, 19, 20, 23, 28, 32),
    "norm": (33, 42),
    "g3": (13, 14, 16, 17, 22, 27, 31, 36),
    "p1": (3, 4, 5, 6, 7, 8, 9, 10),
    "p5": (19, 23, 27, 32, 33, 34, 40, 41),
    "p4": (14, 18, 21, 26, 27, 30, 34, 37),
    "p2": (5, 9, 11, 13, 14, 18, 22, 25),
    "g2": (9, 10, 11, 12, 15, 20, 23, 29),
    "g4": (17, 18, 23, 24, 28, 34, 35, 41),
    "n3": (41, 42, 43, 44, 49, 50, 51, 52),
    "q": (44, 46, 47, 48, 52, 53, 54, 55),
    "w3": (44,),
    "w2": (20, 22, 27, 29, 32, 37, 38, 44),
}
G_XFIRST = (1, 1, 1, 1, 1, 1, 1, 0)
N_XFIRST = (1, 0, 0, 0, 0, 0, 0, 0)
SPAN = 30

RING_STEPS = (2, 2, 1, 3, 0, 1, 3, 0)
OWN_HALF = (0, 1, 0, 0, 0, 1, 1, 1)


def digit(table, j):
    packed = sum(v * 4**i for i, v in enumerate(table))
    scale = (1 + 3 * (j % 2)) * (1 + 15 * ((j // 2) % 2)) * (1 + 255 * (j // 4))
    return (packed // scale) % 4


def wait_for(ref, sem):
    pltpu.make_async_copy(ref, ref, sem).wait()


def kernel(
    ctx_hbm, res_hbm, ow_hbm, bias_hbm, gain_hbm, nbias_hbm, qw_hbm, qbias_hbm, grad_hbm,
    query_hbm, gctx_hbm, gow_hbm,
    ctx, ctxp, ctxt, rest, res, bias, gain, nbias, qbias, wv, xsend, xbuf, pbuf,
    s1r, s1l, finl, finr, ybuf, hbuf,
    wq, gbuf, wbuf, ws1r, ws1l, wfinl, wfinr, wy, gacc, qacc, rowsum, gctx, query,
    in_sem, wv_sem, wq_sem, gin_sem, out_sem,
    xsend_sem, xrecv_sem, p_send, s1r_sem, s1l_sem, finl_sem, finr_sem, y_sem,
    g_send, gc_send, g_sem, gc_sem, n_send, n_sem,
    w_send, ws1_send, ws1r_sem, ws1l_sem, wfinl_sem, wfinr_sem, wy_send, wy_sem,
):
    s = lax.axis_index("section")
    d = lax.axis_index("dp")
    t = lax.axis_index("tensor")
    x, yh = t // 2, t % 2
    yl, z = d // 4, d % 4
    other_core = (1 - s, d, t)
    xr = (s, d, ((x + 1) % 4) * 2 + yh)
    xl = (s, d, ((x + 3) % 4) * 2 + yh)
    ypart = (s, d, x * 2 + (1 - yh))
    zr = (s, yl * 4 + (z + 1) % 4, t)
    zl = (s, yl * 4 + (z + 3) % 4, t)
    pair = (s, (1 - yl) * 4 + z, t)

    def send(src, dst, ssem, rsem, to):
        pltpu.make_async_remote_copy(
            src_ref=src, dst_ref=dst, send_sem=ssem, recv_sem=rsem, device_id=to, device_id_type=MESH
        ).start()

    def own(offset):
        return ((x + offset) % 4) * 2 + yh

    def far(offset):
        return ((x + offset) % 4) * 2 + 1 - yh

    small = [
        pltpu.make_async_copy(ctx_hbm, ctx, in_sem.at[0]),
        pltpu.make_async_copy(gain_hbm, gain, in_sem.at[1]),
        pltpu.make_async_copy(nbias_hbm, nbias, in_sem.at[2]),
        pltpu.make_async_copy(qbias_hbm, qbias, in_sem.at[3]),
        pltpu.make_async_copy(bias_hbm, bias, in_sem.at[4]),
    ] + [
        pltpu.make_async_copy(
            res_hbm.at[q],
            rest.at[q, pl.ds(pl.multiple_of(yh * FEATS, 16), FEATS)],
            in_sem.at[5 + q],
        )
        for q in range(2)
    ]
    rest[...] = jnp.zeros_like(rest)
    for load in small:
        load.start()

    def wv_load(c):
        return pltpu.make_async_copy(
            ow_hbm.at[:, pl.ds(pl.multiple_of(c * CW, 128), CW)], wv.at[c], wv_sem.at[c]
        )

    def gin_load(c):
        return pltpu.make_async_copy(
            grad_hbm.at[:, pl.ds(pl.multiple_of(c * CW, 128), CW)],
            gbuf.at[c, pl.ds(s * SEQ_ROWS + t * PIECE, PIECE)],
            gin_sem.at[c],
        )

    def wq_load(c):
        return pltpu.make_async_copy(
            qw_hbm.at[pl.ds((c % 4) * 2 * CW, 2 * CW)], wq.at[c % WQ_SLOTS], wq_sem.at[c % WQ_SLOTS]
        )

    wv_load(0).start()

    @pl.loop(0, CHUNKS)
    def _(c):
        gin_load(c).start()

    @pl.loop(1, CHUNKS)
    def _(c):
        wv_load(c).start()

    @pl.loop(0, WQ_SLOTS)
    def _(c):
        wq_load(c).start()

    barrier = pltpu.get_barrier_semaphore()
    neighbours = (other_core, xr, xl, ypart, zr, zl, pair)
    for to in neighbours:
        pl.semaphore_signal(barrier, inc=1, device_id=to, device_id_type=MESH)

    gacc[...] = jnp.zeros_like(gacc)
    qacc[...] = jnp.zeros_like(qacc)
    rowsum[...] = jnp.zeros_like(rowsum)
    for load in small:
        load.wait()
    ctxt[...] = ctx[...].T
    for q in range(2):
        by_row = rest[q].T
        for t_ in range(8):
            for h in range(2):
                rows = slice(t_ * PIECE + h * SUB, t_ * PIECE + (h + 1) * SUB)
                ctxp[q, h, t_ * SUB:(t_ + 1) * SUB] = ctx[q * SEQ_ROWS + rows.start:q * SEQ_ROWS + rows.stop]
                res[q, h, t_ * SUB:(t_ + 1) * SUB] = by_row[rows]

    @pl.loop(0, CHUNKS)
    def _(c):
        gin_load(c).wait()

    pl.semaphore_wait(barrier, len(neighbours))

    res_chunk = 4 * s + x

    def pair_of(u):
        return u // 4, pl.ds((u % 4) * 2, 2)

    def product(q, u, finish):
        h = u // 4
        for i in range(2):
            c = (u % 4) * 2 + i
            part = jnp.dot(ctxp[q, h], wv[c], preferred_element_type=F32)

            @pl.when(c == res_chunk)
            def _():
                finish(i, c, part + res[q, h].astype(F32) + bias[...])

            @pl.when(c != res_chunk)
            def _():
                finish(i, c, part)

    def p1(u):
        slot = u % 2

        @pl.when(u < 4)
        def _():
            for i in range(2):
                wv_load(u * 2 + i).wait()

        @pl.when(u >= 2)
        def _():
            wait_for(xsend.at[slot], xsend_sem.at[slot])

        def finish(i, c, part):
            xsend[slot, i] = part.astype(BF16).reshape(8, SUB, CW)

        product(1 - s, u, finish)
        h, chunks = pair_of(u)
        send(xsend.at[slot], xbuf.at[chunks, h], xsend_sem.at[slot], xrecv_sem.at[u], other_core)

    def p2(u):
        h, chunks = pair_of(u)
        wait_for(xbuf.at[chunks, h], xrecv_sem.at[u])

        def finish(i, c, part):
            total = part.reshape(8, SUB, CW) + xbuf[c, h].astype(F32)
            pbuf[c, h] = total.astype(BF16)

        product(s, u, finish)
        send(pbuf.at[chunks, h, far(2)], s1r.at[u], p_send, s1r_sem.at[u], xr)
        send(pbuf.at[chunks, h, own(2)], s1l.at[u], p_send, s1l_sem.at[u], xl)
        send(pbuf.at[chunks, h, own(1)], finl.at[u, 0], p_send, finl_sem.at[u, 0], xr)
        send(pbuf.at[chunks, h, far(3)], finr.at[u, 1], p_send, finr_sem.at[u, 1], xl)

    def p3(u):
        h, chunks = pair_of(u)
        wait_for(s1r.at[u], s1r_sem.at[u])
        piece = far(1)
        pbuf[chunks, h, piece] = (pbuf[chunks, h, piece].astype(F32) + s1r[u].astype(F32)).astype(BF16)
        send(pbuf.at[chunks, h, piece], finl.at[u, 1], p_send, finl_sem.at[u, 1], xr)
        wait_for(s1l.at[u], s1l_sem.at[u])
        piece = own(3)
        pbuf[chunks, h, piece] = (pbuf[chunks, h, piece].astype(F32) + s1l[u].astype(F32)).astype(BF16)
        send(pbuf.at[chunks, h, piece], finr.at[u, 0], p_send, finr_sem.at[u, 0], xl)

    def p4(u):
        h, chunks = pair_of(u)
        wait_for(finl.at[u, 1], finl_sem.at[u, 1])
        wait_for(finr.at[u, 1], finr_sem.at[u, 1])
        piece = far(0)
        pbuf[chunks, h, piece] = (
            pbuf[chunks, h, piece].astype(F32) + finl[u, 1].astype(F32) + finr[u, 1].astype(F32)
        ).astype(BF16)
        send(pbuf.at[chunks, h, piece], ybuf.at[u], p_send, y_sem.at[u], ypart)

    def p5(u):
        h, chunks = pair_of(u)
        wait_for(finl.at[u, 0], finl_sem.at[u, 0])
        wait_for(finr.at[u, 0], finr_sem.at[u, 0])
        wait_for(ybuf.at[u], y_sem.at[u])
        total = (
            pbuf[chunks, h, own(0)].astype(F32)
            + finl[u, 0].astype(F32)
            + finr[u, 0].astype(F32)
            + ybuf[u].astype(F32)
        )
        handoff = total.astype(BF16)
        hbuf[h, chunks] = handoff
        rowsum[h] += jnp.sum(jnp.sum(handoff.astype(F32), axis=0), axis=-1, keepdims=True)

    def gather1(piece, ssem, sem):
        mine = piece(own(0))
        send(mine, mine, ssem, sem(1), xr)
        send(mine, mine, ssem, sem(2), xl)
        send(mine, mine, ssem, sem(0), ypart)

    def gather2(piece, half, ssem, sem, xfirst):
        def pass_on(ref, index, to):
            send(ref, ref, ssem, sem(index), to)

        @pl.when(xfirst == 1)
        def _():
            wait_for(piece(own(3)), sem(1))
            pass_on(half(own(3), 0), 5, xr)
            pass_on(piece(own(3)), 3, ypart)
            wait_for(piece(own(1)), sem(2))
            pass_on(half(own(1), 1), 6, xl)
            pass_on(piece(own(1)), 4, ypart)

        @pl.when(xfirst == 0)
        def _():
            wait_for(piece(own(3)), sem(1))
            pass_on(piece(own(3)), 5, xr)
            wait_for(piece(far(0)), sem(0))
            pass_on(piece(far(0)), 4, xl)
            pass_on(piece(far(0)), 3, xr)

    def gather3(piece, half, ssem, sem, xfirst):
        def pass_on(ref, index, to):
            send(ref, ref, ssem, sem(index), to)

        @pl.when(xfirst == 1)
        def _():
            wait_for(half(own(2), 0), sem(5))
            wait_for(half(own(2), 1), sem(6))
            pass_on(piece(own(2)), 7, ypart)

        @pl.when(xfirst == 0)
        def _():
            wait_for(piece(far(1)), sem(4))
            pass_on(piece(far(1)), 6, xl)

    def gather4(piece, sem, xfirst):
        @pl.when(xfirst == 1)
        def _():
            wait_for(piece(far(0)), sem(0))
            wait_for(piece(far(3)), sem(3))
            wait_for(piece(far(1)), sem(4))
            wait_for(piece(far(2)), sem(7))

        @pl.when(xfirst == 0)
        def _():
            wait_for(piece(own(1)), sem(2))
            wait_for(piece(far(3)), sem(3))
            wait_for(piece(own(2)), sem(5))
            wait_for(piece(far(2)), sem(6))

    def order(j):
        step, mine = digit(RING_STEPS, j), digit(OWN_HALF, j)
        half = (yl + 1 + mine) % 2
        return half * 4 + (z + step) % 4, step, mine

    def g_refs(j):
        c = order(j)[0]

        def piece(device):
            return gbuf.at[c, pl.ds(s * SEQ_ROWS + device * PIECE, PIECE)]

        def half(device, i):
            return gbuf.at[c, pl.ds(s * SEQ_ROWS + device * PIECE + i * SUB, SUB)]

        def sem(i):
            return g_sem.at[j, i]

        return piece, half, sem

    def g1(j):
        piece, half, sem = g_refs(j)
        gather1(piece, g_send, sem)

    def g2(j):
        piece, half, sem = g_refs(j)
        gather2(piece, half, g_send, sem, digit(G_XFIRST, j))

    def g3(j):
        piece, half, sem = g_refs(j)
        gather3(piece, half, g_send, sem, digit(G_XFIRST, j))

    def g4(j):
        piece, half, sem = g_refs(j)
        gather4(piece, sem, digit(G_XFIRST, j))
        rows = pl.ds(s * SEQ_ROWS, SEQ_ROWS)
        c = order(j)[0]
        send(gbuf.at[c, rows], gbuf.at[c, rows], gc_send, gc_sem.at[j], other_core)

    def compute(j):
        c, step, mine = order(j)
        rows = pl.ds((1 - s) * SEQ_ROWS, SEQ_ROWS)
        wait_for(gbuf.at[c, rows], gc_sem.at[j])
        slot = j % 6

        @pl.when(j >= 6)
        def _():
            wait_for(wbuf.at[slot], ws1_send.at[slot])

        term = jnp.dot(ctxt[...], gbuf[c], preferred_element_type=F32).astype(BF16)
        wbuf[slot, 0] = term[:HALF]
        wbuf[slot, 1] = term[HALF:]

        @pl.when(j < 2)
        def _():
            send(wbuf.at[slot, 0], ws1r.at[mine], ws1_send.at[slot], ws1r_sem.at[mine], zr)
            send(wbuf.at[slot, 1], ws1l.at[mine], ws1_send.at[slot], ws1l_sem.at[mine], zl)

        @pl.when(step == 1)
        def _():
            send(wbuf.at[slot, 1], wfinl.at[mine, 1], w_send, wfinl_sem.at[mine, 1], zr)

        @pl.when(step == 3)
        def _():
            send(wbuf.at[slot, 0], wfinr.at[mine, 0], w_send, wfinr_sem.at[mine, 0], zl)

        back = gacc[...] + lax.dot_general(
            gbuf[c], wv[c], (((1,), (1,)), ((), ())), preferred_element_type=F32
        )

        @pl.when(j < CHUNKS - 1)
        def _():
            gacc[...] = back

        @pl.when(j == CHUNKS - 1)
        def _():
            gctx[...] = back.astype(BF16)
            pltpu.make_async_copy(gctx, gctx_hbm, out_sem.at[0]).start()

    def w2(j):
        _, step, mine = order(j)
        slot = j % 6

        @pl.when(step == 1)
        def _():
            wait_for(ws1r.at[mine], ws1r_sem.at[mine])
            wbuf[slot, 0] = (wbuf[slot, 0].astype(F32) + ws1r[mine].astype(F32)).astype(BF16)
            send(wbuf.at[slot, 0], wfinl.at[mine, 0], w_send, wfinl_sem.at[mine, 0], zr)

        @pl.when(step == 3)
        def _():
            wait_for(ws1l.at[mine], ws1l_sem.at[mine])
            wbuf[slot, 1] = (wbuf[slot, 1].astype(F32) + ws1l[mine].astype(F32)).astype(BF16)
            send(wbuf.at[slot, 1], wfinr.at[mine, 1], w_send, wfinr_sem.at[mine, 1], zl)

    def w3(_):
        for half in range(2):
            wait_for(wfinl.at[0, half], wfinl_sem.at[0, half])
            wait_for(wfinr.at[0, half], wfinr_sem.at[0, half])
            wbuf[4, half] = (
                wbuf[4, half].astype(F32) + wfinl[0, half].astype(F32) + wfinr[0, half].astype(F32)
            ).astype(BF16)
            send(wbuf.at[4, half], wy.at[half], wy_send.at[half], wy_sem.at[half], pair)

    def n_refs(u):
        h, chunks = pair_of(u)

        def piece(device):
            return xbuf.at[chunks, h, device]

        def half(device, i):
            return xbuf.at[(u % 4) * 2 + i, h, device]

        def sem(i):
            return n_sem.at[u, i]

        return piece, half, sem

    def norm(h):
        mean = rowsum[h] * (1.0 / WIDTH)

        def square(c, total):
            centred = hbuf[h, c].astype(F32) - mean
            return total + jnp.sum(centred * centred, axis=-1, keepdims=True)

        total = lax.fori_loop(0, CHUNKS, square, jnp.zeros((SUB, 1), F32))
        scale = lax.rsqrt(total * (1.0 / WIDTH) + EPSILON)

        for i in range(4):
            for c in (2 * i, 2 * i + 1):
                centred = hbuf[h, c].astype(F32) - mean
                cols = slice(c * CW, (c + 1) * CW)
                normed = centred * scale * gain[cols].reshape(1, CW) + nbias[cols].reshape(1, CW)
                xbuf[c, h, own(0)] = normed.astype(BF16)
            piece, half, sem = n_refs(h * 4 + i)
            gather1(piece, n_send, sem)

    def n2(u):
        piece, half, sem = n_refs(u)
        gather2(piece, half, n_send, sem, digit(N_XFIRST, u))

    def n3(u):
        piece, half, sem = n_refs(u)
        gather3(piece, half, n_send, sem, digit(N_XFIRST, u))

    def q(u):
        piece, half, sem = n_refs(u)
        gather4(piece, sem, digit(N_XFIRST, u))
        h = u // 4
        wq_load(u).wait()
        slot = u % WQ_SLOTS
        total = qacc[h]
        for i in range(2):
            rows = xbuf[(u % 4) * 2 + i, h].reshape(8 * SUB, CW)
            total += jnp.dot(rows, wq[slot, i * CW:(i + 1) * CW], preferred_element_type=F32)

        @pl.when(u % 4 < 3)
        def _():
            qacc[h] = total

        @pl.when(u % 4 == 3)
        def _():
            full = total + qbias[...].reshape(1, QCOLS)
            query[h] = full.astype(BF16).reshape(8, SUB, QCOLS)
            pltpu.make_async_copy(query.at[h], query_hbm.at[:, h], out_sem.at[2 + h]).start()

        @pl.when(u + WQ_SLOTS < UNITS)
        def _():
            wq_load(u + WQ_SLOTS).start()

    bodies = {
        "g1": g1, "p1": p1, "p2": p2, "p3": p3, "p4": p4, "p5": p5, "g2": g2, "g3": g3, "g4": g4,
        "c": compute, "w2": w2, "w3": w3, "norm": norm, "n2": n2, "n3": n3, "q": q,
    }

    def mask(name, span):
        return sum(1 << (k - span * SPAN) for k in SCHEDULE[name] if k // SPAN == span)

    def tick(k, state):
        later = []
        for i, name in enumerate(SCHEDULE):
            left, index = state[2 * i], state[2 * i + 1]
            active = left % 2

            @pl.when(active == 1)
            def _():
                bodies[name](index)

            left = left // 2
            for span in range(1, spans):
                if mask(name, span):
                    left = left + mask(name, span) * ((k + 1) // (span * SPAN) - k // (span * SPAN))
            later += [left, index + active]
        return tuple(later)

    ticks = 1 + max(max(v) for v in SCHEDULE.values())
    spans = (ticks + SPAN - 1) // SPAN
    start = []
    for name in SCHEDULE:
        start += [jnp.int32(mask(name, 0)), jnp.int32(0)]
    lax.fori_loop(0, ticks, tick, tuple(start))

    for half in range(2):
        wait_for(wfinl.at[1, half], wfinl_sem.at[1, half])
        wait_for(wfinr.at[1, half], wfinr_sem.at[1, half])
        wait_for(wy.at[half], wy_sem.at[half])
        wbuf[1, half] = (
            wbuf[1, half].astype(F32)
            + wfinl[1, half].astype(F32)
            + wfinr[1, half].astype(F32)
            + wy[half].astype(F32)
        ).astype(BF16)
    pltpu.make_async_copy(wbuf.at[1], gow_hbm, out_sem.at[1]).start()

    pltpu.make_async_copy(gctx, gctx_hbm, out_sem.at[0]).wait()
    for h in range(2):
        pltpu.make_async_copy(query.at[h], query_hbm.at[:, h], out_sem.at[2 + h]).wait()
    pltpu.make_async_copy(wbuf.at[1], gow_hbm, out_sem.at[1]).wait()

    for slot in range(2):
        wait_for(xsend.at[slot], xsend_sem.at[slot])
        wait_for(wy.at[slot], wy_send.at[slot])
    wait_for(pbuf.at[:, :, pl.ds(0, 7)], p_send)
    wait_for(gbuf.at[:, pl.ds(0, 224)], g_send)
    wait_for(gbuf.at[:, pl.ds(0, 256)], gc_send)
    wait_for(xbuf.at[:, :, pl.ds(0, 7)], n_send)
    wait_for(wbuf.at[pl.ds(2, 4)], w_send)


def store(*refs):
    sources, results, sems = refs[:3], refs[3:6], refs[6]
    copies = [pltpu.make_async_copy(a, b, sems.at[i]) for i, (a, b) in enumerate(zip(sources, results))]
    for copy in copies:
        copy.start()
    for copy in copies:
        copy.wait()


def local(
    context, residual, out_weight, out_bias, norm_gain, norm_bias, query_weight, query_bias, grad_handoff
):
    rows = 2 * SEQ_ROWS
    yh = lax.axis_index("tensor") % 2
    zero = jnp.zeros_like(out_bias)
    wide_bias = jnp.where(
        yh == 0, jnp.concatenate([out_bias, zero]), jnp.concatenate([zero, out_bias])
    ).reshape(1, CW)

    dma = pltpu.SemaphoreType.DMA
    any_spec = pl.BlockSpec(memory_space=pl.ANY)
    results = (
        jax.ShapeDtypeStruct((8, 2, SUB, QCOLS), BF16),
        jax.ShapeDtypeStruct((rows, HEADS), BF16),
        jax.ShapeDtypeStruct((2, HALF, CW), BF16),
    )
    parts = pl.pallas_call(
        kernel,
        out_shape=results,
        in_specs=[any_spec] * 9,
        out_specs=(any_spec,) * 3,
        scratch_shapes=[
            pltpu.VMEM((rows, HEADS), BF16),
            pltpu.VMEM((2, 2, 8 * SUB, HEADS), BF16),
            pltpu.VMEM((HEADS, rows), BF16),
            pltpu.VMEM((2, CW, SEQ_ROWS), BF16),
            pltpu.VMEM((2, 2, 8 * SUB, CW), BF16),
            pltpu.VMEM((1, CW), F32),
            pltpu.VMEM((WIDTH,), F32),
            pltpu.VMEM((WIDTH,), F32),
            pltpu.VMEM((QCOLS,), F32),
            pltpu.VMEM((CHUNKS, HEADS, CW), BF16),
            pltpu.VMEM((2, 2, 8, SUB, CW), BF16),
            pltpu.VMEM((CHUNKS, 2, 8, SUB, CW), BF16),
            pltpu.VMEM((CHUNKS, 2, 8, SUB, CW), BF16),
            pltpu.VMEM((UNITS, 2, SUB, CW), BF16),
            pltpu.VMEM((UNITS, 2, SUB, CW), BF16),
            pltpu.VMEM((UNITS, 2, 2, SUB, CW), BF16),
            pltpu.VMEM((UNITS, 2, 2, SUB, CW), BF16),
            pltpu.VMEM((UNITS, 2, SUB, CW), BF16),
            pltpu.VMEM((2, CHUNKS, SUB, CW), BF16),
            pltpu.VMEM((WQ_SLOTS, 2 * CW, QCOLS), BF16),
            pltpu.VMEM((CHUNKS, rows, CW), BF16),
            pltpu.VMEM((6, 2, HALF, CW), BF16),
            pltpu.VMEM((2, HALF, CW), BF16),
            pltpu.VMEM((2, HALF, CW), BF16),
            pltpu.VMEM((2, 2, HALF, CW), BF16),
            pltpu.VMEM((2, 2, HALF, CW), BF16),
            pltpu.VMEM((2, HALF, CW), BF16),
            pltpu.VMEM((rows, HEADS), F32),
            pltpu.VMEM((2, 8 * SUB, QCOLS), F32),
            pltpu.VMEM((2, SUB, 1), F32),
            pltpu.VMEM((rows, HEADS), BF16),
            pltpu.VMEM((2, 8, SUB, QCOLS), BF16),
            dma((7,)),
            dma((CHUNKS,)),
            dma((WQ_SLOTS,)),
            dma((CHUNKS,)),
            dma((4,)),
            dma((2,)),
            dma((UNITS,)),
            dma,
            dma((UNITS,)),
            dma((UNITS,)),
            dma((UNITS, 2)),
            dma((UNITS, 2)),
            dma((UNITS,)),
            dma,
            dma,
            dma((CHUNKS, 8)),
            dma((CHUNKS,)),
            dma,
            dma((UNITS, 8)),
            dma,
            dma((2,)),
            dma((2,)),
            dma((2,)),
            dma((2, 2)),
            dma((2, 2)),
            dma((2,)),
            dma((2,)),
        ],
        compiler_params=pltpu.CompilerParams(
            collective_id=0, has_side_effects=True, vmem_limit_bytes=62 * 2**20
        ),
    )(
        context.reshape(rows, HEADS),
        residual.transpose(0, 2, 1),
        out_weight,
        wide_bias,
        norm_gain,
        norm_bias,
        query_weight,
        query_bias,
        grad_handoff.reshape(PIECE, WIDTH),
    )
    query, gctx, gow = pl.pallas_call(
        store,
        out_shape=results,
        in_specs=[pl.BlockSpec(memory_space=pltpu.VMEM)] * 3,
        out_specs=(any_spec,) * 3,
        scratch_shapes=[dma((3,))],
    )(*parts)
    return (
        query.reshape(1, SEQ_ROWS, QCOLS),
        gctx.reshape(2, SEQ_ROWS, HEADS),
        gow.reshape(HEADS, CW),
    )


def solution(mesh):
    in_specs = (
        P(None, "dp", ("section", "tensor")),
        P(None, "dp", ("section", "tensor")),
        P(("section", "tensor"), None),
        P(("section", "tensor")),
        P(),
        P(),
        P(None, "tensor"),
        P("tensor"),
        P("section", ("dp", "tensor"), None),
    )
    out_specs = (
        P("section", "dp", "tensor"),
        P(None, "dp", ("section", "tensor")),
        P(("section", "tensor"), "dp"),
    )
    return jax.shard_map(local, mesh=mesh, in_specs=in_specs, out_specs=out_specs, check_vma=False)
```

```python
import jax
import jax.numpy as jnp
from jax import lax
from jax.experimental import pallas as pl
from jax.experimental.pallas import tpu as pltpu
from jax.sharding import PartitionSpec as P

EPSILON = 1e-05
MESH = pl.DeviceIdType.MESH
BF16 = jnp.bfloat16
F32 = jnp.float32

CHUNKS = 8
CW = 1152
WIDTH = CHUNKS * CW
FEATS = WIDTH // 16
SEQ_ROWS = 256
PIECE = 32
SUB = 16
UNITS = 8
HEADS = 384
HALF = HEADS // 2
QCOLS = 768
WQ_SLOTS = 2

SCHEDULE = {
    "w3": (44,),
    "g1": (0, 1, 2, 3, 4, 5, 7, 29),
    "prep": (3,),
    "prep2": (12,),
    "n2": (36, 37, 38, 39, 44, 45, 46, 47),
    "p2": (7, 8, 11, 13, 15, 17, 18, 22),
    "g2": (7, 9, 11, 12, 14, 18, 22, 38),
    "p1": (4, 5, 6, 7, 8, 9, 10, 11),
    "g4": (16, 18, 20, 22, 27, 31, 35, 46),
    "w2": (19, 25, 27, 28, 30, 35, 36, 50),
    "p5": (22, 23, 26, 32, 35, 39, 40, 41),
    "p4": (15, 16, 18, 28, 32, 33, 34, 35),
    "norm": (32, 41),
    "n3": (39, 40, 41, 42, 48, 49, 50, 51),
    "g3": (12, 13, 14, 15, 20, 26, 31, 41),
    "q": (42, 43, 45, 47, 51, 52, 53, 54),
    "p3": (11, 12, 13, 18, 23, 24, 25, 29),
    "w4": (50, 54),
    "c": (17, 20, 21, 25, 28, 32, 35, 47),
}
G_XFIRST = (1, 1, 1, 1, 1, 1, 1, 0)
N_XFIRST = (1, 0, 0, 0, 0, 0, 0, 0)
SPAN = 30

RING_STEPS = (2, 2, 1, 3, 0, 1, 3, 0)
OWN_HALF = (0, 1, 0, 0, 0, 1, 1, 1)


def digit(table, j):
    packed = sum(v * 4**i for i, v in enumerate(table))
    scale = (1 + 3 * (j % 2)) * (1 + 15 * ((j // 2) % 2)) * (1 + 255 * (j // 4))
    return (packed // scale) % 4


def wait_for(ref, sem):
    pltpu.make_async_copy(ref, ref, sem).wait()


def kernel(
    ctx_hbm, res_hbm, ow_hbm, bias_hbm, gain_hbm, nbias_hbm, qw_hbm, qbias_hbm, grad_hbm,
    query_ref, gctx_ref, gow_ref,
    ctx, ctxp, ctxt, rest, res, bias, wide, gain, nbias, qbias, wv, xsend, xbuf, pbuf,
    s1, fin, hbuf,
    wq, gbuf, wbuf, ws1r, ws1l, wfin, gacc, qacc, rowsum,
    in_sem, wv_sem, wq_sem, gin_sem,
    xsend_sem, xrecv_sem, p_send, s1_sem, fin_sem,
    g_send, gc_send, g_sem, gc_sem, n_send, n_sem,
    w_send, ws1_send, ws1r_sem, ws1l_sem, wfin_sem, wy_send,
):
    s = lax.axis_index("section")
    d = lax.axis_index("dp")
    t = lax.axis_index("tensor")
    x, yh = t // 2, t % 2
    yl, z = d // 4, d % 4
    other_core = (1 - s, d, t)
    xr = (s, d, ((x + 1) % 4) * 2 + yh)
    xl = (s, d, ((x + 3) % 4) * 2 + yh)
    ypart = (s, d, x * 2 + (1 - yh))
    zr = (s, yl * 4 + (z + 1) % 4, t)
    zl = (s, yl * 4 + (z + 3) % 4, t)
    pair = (s, (1 - yl) * 4 + z, t)

    def send(src, dst, ssem, rsem, to):
        pltpu.make_async_remote_copy(
            src_ref=src, dst_ref=dst, send_sem=ssem, recv_sem=rsem, device_id=to, device_id_type=MESH
        ).start()

    def own(offset):
        return ((x + offset) % 4) * 2 + yh

    def far(offset):
        return ((x + offset) % 4) * 2 + 1 - yh

    barrier = pltpu.get_barrier_semaphore()
    neighbours = (other_core, xr, xl, ypart, zr, zl, pair)
    for to in neighbours:
        pl.semaphore_signal(barrier, inc=1, device_id=to, device_id_type=MESH)

    small = [
        pltpu.make_async_copy(ctx_hbm, ctx, in_sem.at[0]),
        pltpu.make_async_copy(gain_hbm, gain, in_sem.at[1]),
        pltpu.make_async_copy(nbias_hbm, nbias, in_sem.at[2]),
        pltpu.make_async_copy(qbias_hbm, qbias, in_sem.at[3]),
        pltpu.make_async_copy(bias_hbm, bias, in_sem.at[4]),
    ] + [
        pltpu.make_async_copy(
            res_hbm.at[q],
            rest.at[q, pl.ds(pl.multiple_of(yh * FEATS, 16), FEATS)],
            in_sem.at[5 + q],
        )
        for q in range(2)
    ]
    for load in small:
        load.start()

    def wv_load(c):
        return pltpu.make_async_copy(
            ow_hbm.at[:, pl.ds(pl.multiple_of(c * CW, 128), CW)], wv.at[c], wv_sem.at[c // 2]
        )

    def gin_load(c):
        return pltpu.make_async_copy(
            grad_hbm.at[:, pl.ds(pl.multiple_of(c * CW, 128), CW)],
            gbuf.at[c, pl.ds(s * SEQ_ROWS + t * PIECE, PIECE)],
            gin_sem,
        )

    def wq_load(c):
        return pltpu.make_async_copy(
            qw_hbm.at[pl.ds((c % 4) * 2 * CW, 2 * CW)], wq.at[c % WQ_SLOTS], wq_sem.at[c % WQ_SLOTS]
        )

    @pl.loop(0, CHUNKS)
    def _(c):
        gin_load(c).start()

    wv_load(0).start()

    @pl.loop(1, CHUNKS)
    def _(c):
        wv_load(c).start()

    @pl.loop(0, WQ_SLOTS)
    def _(c):
        wq_load(c).start()

    wait_for(gbuf.at[:, pl.ds(0, PIECE)], gin_sem)
    pl.semaphore_wait(barrier, len(neighbours))

    def prep(_):
        for load in small:
            load.wait()
        edge = bias[...].reshape(1, FEATS)
        blank = jnp.zeros_like(edge)

        @pl.when(yh == 0)
        def _():
            wide[...] = jnp.concatenate([edge, blank], axis=1)

        @pl.when(yh == 1)
        def _():
            wide[...] = jnp.concatenate([blank, edge], axis=1)

        for q in range(2):
            rest[q, pl.ds(pl.multiple_of((1 - yh) * FEATS, 16), FEATS)] = jnp.zeros(
                (FEATS, SEQ_ROWS), BF16
            )
            by_row = rest[q].T
            for t_ in range(8):
                for h in range(2):
                    rows = slice(t_ * PIECE + h * SUB, t_ * PIECE + (h + 1) * SUB)
                    ctxp[q, h, t_ * SUB:(t_ + 1) * SUB] = ctx[
                        q * SEQ_ROWS + rows.start:q * SEQ_ROWS + rows.stop
                    ]
                    res[q, h, t_ * SUB:(t_ + 1) * SUB] = by_row[rows]

    def prep2(_):
        gacc[...] = jnp.zeros_like(gacc)
        qacc[...] = jnp.zeros_like(qacc)
        rowsum[...] = jnp.zeros_like(rowsum)
        ctxt[...] = ctx[...].T

    res_chunk = 4 * s + x

    def pair_of(u):
        return u // 4, pl.ds((u % 4) * 2, 2)

    def product(q, u, finish):
        h = u // 4
        for i in range(2):
            c = (u % 4) * 2 + i
            part = jnp.dot(ctxp[q, h], wv[c], preferred_element_type=F32)

            @pl.when(c == res_chunk)
            def _():
                finish(i, c, part + res[q, h].astype(F32) + wide[...])

            @pl.when(c != res_chunk)
            def _():
                finish(i, c, part)

    def p1(u):
        slot = u % 2

        @pl.when(u < 4)
        def _():
            wait_for(wv.at[pair_of(u)[1]], wv_sem.at[u])

        @pl.when(u >= 2)
        def _():
            wait_for(xsend.at[slot], xsend_sem.at[slot])

        def finish(i, c, part):
            xsend[slot, i] = part.astype(BF16).reshape(8, SUB, CW)

        product(1 - s, u, finish)
        h, chunks = pair_of(u)
        send(xsend.at[slot], xbuf.at[chunks, h], xsend_sem.at[slot], xrecv_sem.at[u], other_core)

    def p2(u):
        h, chunks = pair_of(u)
        wait_for(xbuf.at[chunks, h], xrecv_sem.at[u])

        def finish(i, c, part):
            total = part.reshape(8, SUB, CW) + xbuf[c, h].astype(F32)
            pbuf[c, h] = total.astype(BF16)

        product(s, u, finish)
        send(pbuf.at[chunks, h, far(2)], s1.at[u, 0], p_send, s1_sem.at[u], xr)
        send(pbuf.at[chunks, h, own(2)], s1.at[u, 1], p_send, s1_sem.at[u], xl)
        send(pbuf.at[chunks, h, own(1)], fin.at[u, 0, 0], p_send, fin_sem.at[u, 0], xr)
        send(pbuf.at[chunks, h, far(3)], fin.at[u, 1, 1], p_send, fin_sem.at[u, 1], xl)

    def p3(u):
        h, chunks = pair_of(u)
        wait_for(s1.at[u], s1_sem.at[u])
        piece = far(1)
        pbuf[chunks, h, piece] = (pbuf[chunks, h, piece].astype(F32) + s1[u, 0].astype(F32)).astype(BF16)
        send(pbuf.at[chunks, h, piece], fin.at[u, 1, 0], p_send, fin_sem.at[u, 1], xr)
        piece = own(3)
        pbuf[chunks, h, piece] = (pbuf[chunks, h, piece].astype(F32) + s1[u, 1].astype(F32)).astype(BF16)
        send(pbuf.at[chunks, h, piece], fin.at[u, 0, 1], p_send, fin_sem.at[u, 0], xl)

    def p4(u):
        h, chunks = pair_of(u)
        wait_for(fin.at[u, 1, pl.ds(0, 2)], fin_sem.at[u, 1])
        piece = far(0)
        pbuf[chunks, h, piece] = (
            pbuf[chunks, h, piece].astype(F32) + fin[u, 1, 0].astype(F32) + fin[u, 1, 1].astype(F32)
        ).astype(BF16)
        send(pbuf.at[chunks, h, piece], fin.at[u, 0, 2], p_send, fin_sem.at[u, 0], ypart)

    def p5(u):
        h, chunks = pair_of(u)
        wait_for(fin.at[u, 0], fin_sem.at[u, 0])
        total = (
            pbuf[chunks, h, own(0)].astype(F32)
            + fin[u, 0, 0].astype(F32)
            + fin[u, 0, 1].astype(F32)
            + fin[u, 0, 2].astype(F32)
        )
        handoff = total.astype(BF16)
        hbuf[h, chunks] = handoff
        rowsum[h] += jnp.sum(jnp.sum(handoff.astype(F32), axis=0), axis=-1, keepdims=True)

    def gather1(piece, ssem, sem, xfirst, ydev):
        mine = piece(own(0))
        send(mine, mine, ssem, sem(0), xr)
        send(mine, mine, ssem, sem(3 - 2 * xfirst), xl)
        send(mine, mine, ssem, sem(1 + 2 * xfirst), ydev)

    def gather2(piece, half, ssem, sem, xfirst, ydev):
        def pass_on(ref, index, to):
            send(ref, ref, ssem, sem(index), to)

        @pl.when(xfirst == 1)
        def _():
            wait_for(piece(own(3)), sem(0))
            pass_on(half(own(3), 0), 2, xr)
            pass_on(piece(own(3)), 3, ydev)
            wait_for(piece(own(1)), sem(1))
            pass_on(half(own(1), 1), 2, xl)
            pass_on(piece(own(1)), 3, ydev)

        @pl.when(xfirst == 0)
        def _():
            wait_for(piece(own(3)), sem(0))
            pass_on(piece(own(3)), 3, xr)
            wait_for(piece(far(0)), sem(1))
            pass_on(piece(far(0)), 2, xl)
            pass_on(piece(far(0)), 3, xr)

    def gather3(piece, ssem, sem, xfirst, ydev):
        def pass_on(ref, index, to):
            send(ref, ref, ssem, sem(index), to)

        @pl.when(xfirst == 1)
        def _():
            wait_for(piece(own(2)), sem(2))
            pass_on(piece(own(2)), 3, ydev)

        @pl.when(xfirst == 0)
        def _():
            wait_for(piece(far(1)), sem(2))
            pass_on(piece(far(1)), 3, xl)

    def gather4(four, sem):
        wait_for(four, sem(3))

    def order(j):
        step, mine = digit(RING_STEPS, j), digit(OWN_HALF, j)
        half = (yl + 1 + mine) % 2
        return half * 4 + (z + step) % 4, step, mine

    def g_refs(j):
        c = order(j)[0]

        def piece(device):
            return gbuf.at[c, pl.ds(s * SEQ_ROWS + device * PIECE, PIECE)]

        def half(device, i):
            return gbuf.at[c, pl.ds(s * SEQ_ROWS + device * PIECE + i * SUB, SUB)]

        def sem(i):
            return g_sem.at[j, i]

        return piece, half, sem, digit(G_XFIRST, j)

    def g1(j):
        piece, half, sem, xfirst = g_refs(j)
        gather1(piece, g_send, sem, xfirst, ypart)

    def g2(j):
        piece, half, sem, xfirst = g_refs(j)
        gather2(piece, half, g_send, sem, xfirst, ypart)

    def g3(j):
        piece, half, sem, xfirst = g_refs(j)
        gather3(piece, g_send, sem, xfirst, ypart)

    def g4(j):
        piece, half, sem, xfirst = g_refs(j)
        c = order(j)[0]
        gather4(gbuf.at[c, pl.ds(0, 4 * PIECE)], sem)
        rows = pl.ds(s * SEQ_ROWS, SEQ_ROWS)
        send(gbuf.at[c, rows], gbuf.at[c, rows], gc_send, gc_sem.at[j], other_core)

    def compute(j):
        c, step, mine = order(j)
        rows = pl.ds((1 - s) * SEQ_ROWS, SEQ_ROWS)
        wait_for(gbuf.at[c, rows], gc_sem.at[j])
        slot = j % 6

        @pl.when(j >= 6)
        def _():
            wait_for(wbuf.at[slot], ws1_send.at[slot])

        term = jnp.dot(ctxt[...], gbuf[c], preferred_element_type=F32).astype(BF16)
        wbuf[slot, 0] = term[:HALF]
        wbuf[slot, 1] = term[HALF:]

        @pl.when(j < 2)
        def _():
            send(wbuf.at[slot, 0], ws1r.at[mine], ws1_send.at[slot], ws1r_sem.at[mine], zr)
            send(wbuf.at[slot, 1], ws1l.at[mine], ws1_send.at[slot], ws1l_sem.at[mine], zl)

        @pl.when(step == 1)
        def _():
            send(wbuf.at[slot, 1], wfin.at[mine, 1, 0], w_send, wfin_sem.at[mine, 1], zr)

        @pl.when(step == 3)
        def _():
            send(wbuf.at[slot, 0], wfin.at[mine, 0, 1], w_send, wfin_sem.at[mine, 0], zl)

        back = gacc[...] + lax.dot_general(
            gbuf[c], wv[c], (((1,), (1,)), ((), ())), preferred_element_type=F32
        )

        @pl.when(j < CHUNKS - 1)
        def _():
            gacc[...] = back

        @pl.when(j == CHUNKS - 1)
        def _():
            gctx_ref[...] = back.astype(BF16)

    def w2(j):
        _, step, mine = order(j)
        slot = j % 6

        @pl.when(step == 1)
        def _():
            wait_for(ws1r.at[mine], ws1r_sem.at[mine])
            wbuf[slot, 0] = (wbuf[slot, 0].astype(F32) + ws1r[mine].astype(F32)).astype(BF16)
            send(wbuf.at[slot, 0], wfin.at[mine, 0, 0], w_send, wfin_sem.at[mine, 0], zr)

        @pl.when(step == 3)
        def _():
            wait_for(ws1l.at[mine], ws1l_sem.at[mine])
            wbuf[slot, 1] = (wbuf[slot, 1].astype(F32) + ws1l[mine].astype(F32)).astype(BF16)
            send(wbuf.at[slot, 1], wfin.at[mine, 1, 1], w_send, wfin_sem.at[mine, 1], zl)

    def w3(_):
        for half in range(2):
            wait_for(wfin.at[0, half, pl.ds(0, 2)], wfin_sem.at[0, half])
            wbuf[4, half] = (
                wbuf[4, half].astype(F32) + wfin[0, half, 0].astype(F32) + wfin[0, half, 1].astype(F32)
            ).astype(BF16)
            send(wbuf.at[4, half], wfin.at[1, half, 2], wy_send.at[half], wfin_sem.at[1, half], pair)

    def w4(half):
        wait_for(wfin.at[1, half], wfin_sem.at[1, half])
        gow_ref[half] = (
            wbuf[1, half].astype(F32)
            + wfin[1, half, 0].astype(F32)
            + wfin[1, half, 1].astype(F32)
            + wfin[1, half, 2].astype(F32)
        ).astype(BF16)

    def n_refs(u):
        h, chunks = pair_of(u)

        def piece(device):
            return xbuf.at[chunks, h, device]

        def half(device, i):
            return xbuf.at[(u % 4) * 2 + i, h, device]

        def sem(i):
            return n_sem.at[u, i]

        return piece, half, sem, digit(N_XFIRST, u)

    def norm(h):
        mean = rowsum[h] * (1.0 / WIDTH)

        def square(c, total):
            centred = hbuf[h, c].astype(F32) - mean
            return total + jnp.sum(centred * centred, axis=-1, keepdims=True)

        total = lax.fori_loop(0, CHUNKS, square, jnp.zeros((SUB, 1), F32))
        scale = lax.rsqrt(total * (1.0 / WIDTH) + EPSILON)

        for i in range(4):
            for c in (2 * i, 2 * i + 1):
                centred = hbuf[h, c].astype(F32) - mean
                cols = slice(c * CW, (c + 1) * CW)
                normed = centred * scale * gain[cols].reshape(1, CW) + nbias[cols].reshape(1, CW)
                xbuf[c, h, own(0)] = normed.astype(BF16)
            piece, half, sem, xfirst = n_refs(h * 4 + i)
            gather1(piece, n_send, sem, xfirst, ypart)

    def n2(u):
        piece, half, sem, xfirst = n_refs(u)
        gather2(piece, half, n_send, sem, xfirst, ypart)

    def n3(u):
        piece, half, sem, xfirst = n_refs(u)
        gather3(piece, n_send, sem, xfirst, ypart)

    def q(u):
        piece, half, sem, xfirst = n_refs(u)
        chunks = pair_of(u)[1]
        gather4(xbuf.at[chunks, 0, pl.ds(0, 4)], sem)
        h = u // 4
        wq_load(u).wait()
        slot = u % WQ_SLOTS
        total = qacc[h]
        for i in range(2):
            rows = xbuf[(u % 4) * 2 + i, h].reshape(8 * SUB, CW)
            total += jnp.dot(rows, wq[slot, i * CW:(i + 1) * CW], preferred_element_type=F32)

        @pl.when(u % 4 < 3)
        def _():
            qacc[h] = total

        @pl.when(u % 4 == 3)
        def _():
            full = total + qbias[...].reshape(1, QCOLS)
            query_ref[:, h] = full.astype(BF16).reshape(8, SUB, QCOLS)

        @pl.when(u + WQ_SLOTS < UNITS)
        def _():
            wq_load(u + WQ_SLOTS).start()

    bodies = {
        "g1": g1, "p1": p1, "p2": p2, "p3": p3, "p4": p4, "p5": p5, "g2": g2, "g3": g3, "g4": g4,
        "c": compute, "w2": w2, "w3": w3, "w4": w4, "prep": prep, "prep2": prep2, "norm": norm, "n2": n2, "n3": n3, "q": q,
    }

    def mask(name, span):
        return sum(1 << (k - span * SPAN) for k in SCHEDULE[name] if k // SPAN == span)

    def tick(k, state):
        later = []
        for i, name in enumerate(SCHEDULE):
            left, index = state[2 * i], state[2 * i + 1]
            active = left % 2

            @pl.when(active == 1)
            def _():
                bodies[name](index)

            left = left // 2
            for span in range(1, spans):
                if mask(name, span):
                    turn = ((k + 1) // (span * SPAN) - k // (span * SPAN)) * (1 - k // (span * SPAN))
                    left = left + mask(name, span) * turn
            later += [left, index + active]
        return tuple(later)

    ticks = 1 + max(max(v) for v in SCHEDULE.values())
    spans = (ticks + SPAN - 1) // SPAN
    start = []
    for name in SCHEDULE:
        start += [jnp.int32(mask(name, 0)), jnp.int32(0)]
    lax.fori_loop(0, ticks, tick, tuple(start))

    for slot in range(2):
        wait_for(xsend.at[slot], xsend_sem.at[slot])
        wait_for(wbuf.at[4, slot], wy_send.at[slot])
    wait_for(pbuf.at[:, :, pl.ds(0, 7)], p_send)
    wait_for(gbuf.at[:, pl.ds(0, 224)], g_send)
    wait_for(gbuf.at[:, pl.ds(0, 256)], gc_send)
    wait_for(xbuf.at[:, :, pl.ds(0, 7)], n_send)
    wait_for(wbuf.at[pl.ds(2, 4)], w_send)


def store(*refs):
    sources, results, sems = refs[:3], refs[3:6], refs[6]
    copies = [pltpu.make_async_copy(a, b, sems.at[i]) for i, (a, b) in enumerate(zip(sources, results))]
    for copy in copies:
        copy.start()
    for copy in copies:
        copy.wait()


def local(
    context, residual, out_weight, out_bias, norm_gain, norm_bias, query_weight, query_bias, grad_handoff
):
    rows = 2 * SEQ_ROWS

    dma = pltpu.SemaphoreType.DMA
    any_spec = pl.BlockSpec(memory_space=pl.ANY)
    shapes = ((8, 2, SUB, QCOLS), (rows, HEADS), (2, HALF, CW))
    parts = pl.pallas_call(
        kernel,
        out_shape=tuple(pltpu.VMEM(shape, BF16) for shape in shapes),
        in_specs=[any_spec] * 9,
        out_specs=(pl.BlockSpec(memory_space=pltpu.VMEM),) * 3,
        scratch_shapes=[
            pltpu.VMEM((rows, HEADS), BF16),
            pltpu.VMEM((2, 2, 8 * SUB, HEADS), BF16),
            pltpu.VMEM((HEADS, rows), BF16),
            pltpu.VMEM((2, CW, SEQ_ROWS), BF16),
            pltpu.VMEM((2, 2, 8 * SUB, CW), BF16),
            pltpu.VMEM((FEATS,), F32),
            pltpu.VMEM((1, CW), F32),
            pltpu.VMEM((WIDTH,), F32),
            pltpu.VMEM((WIDTH,), F32),
            pltpu.VMEM((QCOLS,), F32),
            pltpu.VMEM((CHUNKS, HEADS, CW), BF16),
            pltpu.VMEM((2, 2, 8, SUB, CW), BF16),
            pltpu.VMEM((CHUNKS, 2, 8, SUB, CW), BF16),
            pltpu.VMEM((CHUNKS, 2, 8, SUB, CW), BF16),
            pltpu.VMEM((UNITS, 2, 2, SUB, CW), BF16),
            pltpu.VMEM((UNITS, 2, 3, 2, SUB, CW), BF16),
            pltpu.VMEM((2, CHUNKS, SUB, CW), BF16),
            pltpu.VMEM((WQ_SLOTS, 2 * CW, QCOLS), BF16),
            pltpu.VMEM((CHUNKS, rows, CW), BF16),
            pltpu.VMEM((6, 2, HALF, CW), BF16),
            pltpu.VMEM((2, HALF, CW), BF16),
            pltpu.VMEM((2, HALF, CW), BF16),
            pltpu.VMEM((2, 2, 3, HALF, CW), BF16),
            pltpu.VMEM((rows, HEADS), F32),
            pltpu.VMEM((2, 8 * SUB, QCOLS), F32),
            pltpu.VMEM((2, SUB, 1), F32),
            dma((7,)),
            dma((CHUNKS // 2,)),
            dma((WQ_SLOTS,)),
            dma,
            dma((2,)),
            dma((UNITS,)),
            dma,
            dma((UNITS,)),
            dma((UNITS, 2)),
            dma,
            dma,
            dma((CHUNKS, 4)),
            dma((CHUNKS,)),
            dma,
            dma((UNITS, 4)),
            dma,
            dma((2,)),
            dma((2,)),
            dma((2,)),
            dma((2, 2)),
            dma((2,)),
        ],
        compiler_params=pltpu.CompilerParams(
            collective_id=0, has_side_effects=True, vmem_limit_bytes=58 * 2**20
        ),
    )(
        context.reshape(rows, HEADS),
        residual.transpose(0, 2, 1),
        out_weight,
        out_bias,
        norm_gain,
        norm_bias,
        query_weight,
        query_bias,
        grad_handoff.reshape(PIECE, WIDTH),
    )
    query, gctx, gow = pl.pallas_call(
        store,
        out_shape=tuple(jax.ShapeDtypeStruct(shape, BF16) for shape in shapes),
        in_specs=[pl.BlockSpec(memory_space=pltpu.VMEM)] * 3,
        out_specs=(any_spec,) * 3,
        scratch_shapes=[dma((3,))],
        compiler_params=pltpu.CompilerParams(vmem_limit_bytes=4 * 2**20),
    )(*parts)
    return (
        query.reshape(1, SEQ_ROWS, QCOLS),
        gctx.reshape(2, SEQ_ROWS, HEADS),
        gow.reshape(HEADS, CW),
    )


def solution(mesh):
    in_specs = (
        P(None, "dp", ("section", "tensor")),
        P(None, "dp", ("section", "tensor")),
        P(("section", "tensor"), None),
        P(("section", "tensor")),
        P(),
        P(),
        P(None, "tensor"),
        P("tensor"),
        P("section", ("dp", "tensor"), None),
    )
    out_specs = (
        P("section", "dp", "tensor"),
        P(None, "dp", ("section", "tensor")),
        P(("section", "tensor"), "dp"),
    )
    return jax.shard_map(local, mesh=mesh, in_specs=in_specs, out_specs=out_specs, check_vma=False)
```
